32 devices in a mesh: grp: 4 (over z), src: 4 (over y, x), rcv: 2 (over core).
Axes of the slice: x: 2, y: 2, z: 4, core: 2. Of those that a mesh axis runs over, the one named last changes fastest.
Arguments:
- recorded: bfloat16 [4, 2, 4096, 4096], P('grp', None, 'src', 'rcv'), parts along dimension 0, as said below
- aperture: int32 [128, 32, 3], P(('grp', 'src'), 'rcv'), parts along dimension 0, may hold values from 0 to 32, as said below
Outputs:
- multiples: float32 [4, 2, 4096, 4096], P('grp', None, 'src', 'rcv'), parts along dimension 0
The draws below stay inside these ranges and needn't reach their ends.
There are 4 independent parts, one for each index of `grp`. The reference program is written for one: setup_inputs(seed, part) draws one part's arguments, and reference() takes and returns one part's arrays. A program takes and returns all parts, laid end to end along the dimension named above; each array names one. Nothing has to cross between parts.
Inputs may be any that keep to these rules, and one draw needn't show every extreme that they name: The data obey reciprocity: recorded(f, c, q, j) equals recorded(f, c, j, q). `aperture`: field 1 is from 4 to 32, field 0 plus field 1 is at most 32, field 2 is from 0 to 2. In every draw some tile pair spans all 32 k-blocks and some has taper width 2.
All inputs are finite; a program needn't handle non-finite values.
Results may differ from the reference program's by a relative error of at most 0.0004.
Values may be sent and summed in bfloat16 or wider, within the bound.
A program may use at most 192 MiB of HBM per device.

```python
import jax
import jax.numpy as jnp
from jax import lax

NB = 32
TILE = 128
FREQ = 1
LMIN = 4
TAPER_MAX = 2
N = 4096


def draw_recorded(key, part):
    noise = jax.random.normal(key, (FREQ, 2, N, N), jnp.float32)
    noise = jnp.clip(noise, -4.0, 4.0)
    return ((noise + jnp.swapaxes(noise, 2, 3)) * 0.088).astype(jnp.bfloat16)


def draw_aperture(key, part):
    keys = jax.random.split(key, 5)
    extent = jax.random.randint(keys[0], (NB * NB,), LMIN, NB + 1)
    places = jnp.arange(NB * NB, dtype=jnp.int32)
    widest = jax.random.randint(keys[1], (), 0, NB * NB)
    extent = jnp.where(places == widest, NB, extent)
    lowest = jax.random.randint(keys[2], (NB * NB,), 0, NB - extent + 1)
    taper_width = jax.random.randint(keys[3], (NB * NB,), 0, TAPER_MAX + 1)
    steepest = jax.random.randint(keys[4], (), 0, NB * NB)
    taper_width = jnp.where(places == steepest, TAPER_MAX, taper_width)
    fields = jnp.stack([lowest, extent, taper_width], axis=-1)
    return fields.reshape(NB, NB, 3).astype(jnp.int32)


def setup_inputs(seed: int = 0, part: int = 0) -> dict:
    splits = jax.random.split(jax.random.key(seed), 3)
    part_keys = jax.random.split(jax.random.fold_in(splits[2], part), 3)
    return {
        "recorded": draw_recorded(jax.random.fold_in(jax.random.fold_in(splits[2], part), 71), part),
        "aperture": draw_aperture(jax.random.fold_in(jax.random.fold_in(splits[2], part), 71), part),
    }


def tile_weights(aperture):
    block_ids = jnp.arange(NB, dtype=jnp.int32)
    offset = block_ids[None, None, :] - aperture[..., 0:1]
    extent = aperture[..., 1:2]
    taper_width = aperture[..., 2:3]
    margin = jnp.minimum(offset, extent - 1 - offset)
    ramped = jnp.minimum(1.0, (margin + 1).astype(jnp.float32) / (taper_width + 1).astype(jnp.float32))
    return jnp.where((offset >= 0) & (offset < extent), ramped, 0.0).astype(jnp.float32)


def reference(recorded, aperture):
    weights = tile_weights(aperture)
    right_side = recorded.astype(jnp.float32).reshape(FREQ, 2, N, NB, TILE)

    def source_row(tile_index):
        panel = lax.dynamic_slice_in_dim(recorded, tile_index * TILE, TILE, 2)
        row_weight = jnp.repeat(lax.dynamic_index_in_dim(weights, tile_index, 0, keepdims=False), TILE, axis=1)
        scaled = (panel[:, :, None, :, :].astype(jnp.float32) * row_weight[None, None, :, None, :]).astype(jnp.bfloat16)
        products = jnp.einsum("fatik,fbktj->fabtij", scaled.astype(jnp.float32), right_side, precision=lax.Precision.HIGHEST)
        real_part = products[:, 0, 0] - products[:, 1, 1]
        imag_part = products[:, 0, 1] + products[:, 1, 0]
        stacked = jnp.stack([real_part, imag_part], 1)
        return stacked.transpose(0, 1, 3, 2, 4).reshape(FREQ, 2, TILE, N)

    stacked_rows = lax.map(source_row, jnp.arange(NB, dtype=jnp.int32))
    return stacked_rows.transpose(1, 2, 0, 3, 4).reshape(FREQ, 2, N, N)
```

```python
import functools

import jax
import jax.numpy as jnp
import numpy as np
from jax import lax
from jax.experimental import pallas as pl
from jax.experimental.pallas import tpu as pltpu
from jax.sharding import PartitionSpec as P

TILE = 128
COPIES = 14


def exchange_kernel(x_ref, g_ref, send_sems, recv_sems, local_sem):
    strip = x_ref.shape[2]
    half = strip // 2
    s = lax.axis_index("src")
    r = lax.axis_index("rcv")
    a = s + 1 - 2 * lax.rem(s, 2)
    b = lax.rem(s + 2, 4)
    d = 3 - s
    to_x, to_y, to_sibling = {"src": a}, {"src": b}, {"rcv": 1 - r}
    home = r == s // 2

    def place(u, t, rows=(0, strip), cols=(0, strip)):
        return g_ref.at[
            :,
            pl.ds(pl.multiple_of(u * strip + rows[0], half), rows[1]),
            pl.ds(pl.multiple_of(t * strip + cols[0], half), cols[1]),
        ]

    def own(t, rows=(0, strip), cols=(0, strip)):
        return x_ref.at[
            0,
            :,
            pl.ds(rows[0], rows[1]),
            pl.ds(pl.multiple_of(lax.rem(t, 2) * strip + cols[0], half), cols[1]),
        ]

    def copy(number, source, target, device):
        return pltpu.make_async_remote_copy(
            src_ref=source,
            dst_ref=target,
            send_sem=send_sems.at[number],
            recv_sem=recv_sems.at[number],
            device_id=device,
            device_id_type=pl.DeviceIdType.MESH,
        )

    def arrive(number, target, device):
        copy(number, target, target, device).wait_recv()

    lower, upper = (0, half), (half, half)
    barrier = pltpu.get_barrier_semaphore()
    for device in (to_x, to_y, to_sibling):
        pl.semaphore_signal(barrier, inc=1, device_id=device, device_id_type=pl.DeviceIdType.MESH)
    pl.semaphore_wait(barrier, 3)

    def own_place(core):
        return g_ref.at[
            :,
            pl.ds(pl.multiple_of(s * strip, strip), strip),
            pl.ds(pl.multiple_of(core * 2 * strip, strip), 2 * strip),
        ]

    @pl.when(home)
    def _():
        sends = [
            copy(1, own(s, upper), place(s, s, upper), to_x),
            copy(3, own(s, lower), place(s, s, lower), to_y),
            copy(2, own(s, lower), place(s, s, lower), to_x),
            copy(4, own(s, upper), place(s, s, upper), to_y),
            copy(5, own(a), place(s, a), to_y),
            copy(0, x_ref.at[0], own_place(r), to_sibling),
        ]
        for send in sends:
            send.start()
        local = pltpu.make_async_copy(x_ref.at[0], own_place(r), local_sem)
        local.start()
        arrive(1, place(a, a, upper), to_x)
        forward = copy(6, place(a, a, upper), place(a, a, upper), to_y)
        forward.start()
        arrive(9, place(b, a, cols=upper), to_y)
        share = copy(11, place(b, a, cols=upper), place(b, a, cols=upper), to_sibling)
        share.start()
        arrive(0, own_place(1 - r), to_sibling)
        arrive(2, place(a, a, lower), to_x)
        arrive(12, place(a, d), to_sibling)
        arrive(13, place(a, b, lower), to_sibling)
        local.wait()
        for send in sends + [forward, share]:
            send.wait_send()

    @pl.when(jnp.logical_not(home))
    def _():
        sends = [
            copy(9, own(d, cols=upper), place(s, d, cols=upper), to_y),
            copy(7, own(b), place(s, b), to_x),
            copy(8, own(d, lower), place(s, d, lower), to_x),
            copy(0, x_ref.at[0], own_place(r), to_sibling),
        ]
        for send in sends:
            send.start()
        local = pltpu.make_async_copy(x_ref.at[0], own_place(r), local_sem)
        local.start()
        arrive(3, place(b, b, lower), to_y)
        forward = copy(10, place(b, b, lower), place(b, b, lower), to_x)
        forward.start()
        arrive(7, place(a, d), to_x)
        share = copy(12, place(a, d), place(a, d), to_sibling)
        share.start()
        arrive(8, place(a, b, lower), to_x)
        share_half = copy(13, place(a, b, lower), place(a, b, lower), to_sibling)
        share_half.start()
        arrive(0, own_place(1 - r), to_sibling)
        arrive(11, place(b, a, cols=upper), to_sibling)
        arrive(4, place(b, b, upper), to_y)
        arrive(5, place(b, d), to_y)
        arrive(6, place(d, d, upper), to_y)
        arrive(10, place(d, d, lower), to_x)
        local.wait()
        for send in sends + [forward, share, share_half]:
            send.wait_send()


def exchange(recorded):
    strip = recorded.shape[2]
    whole = 4 * strip
    return pl.pallas_call(
        exchange_kernel,
        out_shape=jax.ShapeDtypeStruct((2, whole, whole), recorded.dtype),
        in_specs=[pl.BlockSpec(memory_space=pl.ANY)],
        out_specs=pl.BlockSpec(memory_space=pl.ANY),
        scratch_shapes=[
            pltpu.SemaphoreType.DMA((COPIES,)),
            pltpu.SemaphoreType.DMA((COPIES,)),
            pltpu.SemaphoreType.DMA,
        ],
        compiler_params=pltpu.CompilerParams(collective_id=0, has_side_effects=True),
        name="exchange",
    )(recorded)


def apply_kernel(
    row_tiles, col_tiles, blocks, mixed, aperture, straight, places, left_ref, *refs
):
    if mixed:
        column_ref, row_ref, out_ref, lhs, rhs, acc = refs
    else:
        column_ref, out_ref, lhs, rhs, acc = refs
    j = pl.program_id(0)

    def span(block, count):
        return pl.ds(pl.multiple_of(block * (2 * TILE), 2 * TILE), count * 2 * TILE)

    @pl.when(j == 0)
    def _():
        def interleave(k, carry):
            for c in range(2):
                lhs[:, pl.ds(pl.multiple_of((2 * k + c) * TILE, TILE), TILE)] = left_ref[
                    c, :, pl.ds(pl.multiple_of(k * TILE, TILE), TILE)
                ]
            return carry

        lax.fori_loop(0, blocks, interleave, 0)

    def build(k, carry):
        here = pl.ds(pl.multiple_of(k * TILE, TILE), TILE)
        first = pl.ds(pl.multiple_of(k * 2 * TILE, TILE), TILE)
        second = pl.ds(pl.multiple_of(k * 2 * TILE + TILE, TILE), TILE)

        def fill(real, imag):
            rhs[first, :TILE] = real
            rhs[first, TILE:] = imag
            rhs[second, :TILE] = -imag
            rhs[second, TILE:] = real

        if not mixed:
            fill(column_ref[0, here, :], column_ref[1, here, :])
            return carry
        as_is = straight[k * col_tiles + j] == 1

        @pl.when(as_is)
        def _():
            fill(column_ref[0, here, :], column_ref[1, here, :])

        @pl.when(jnp.logical_not(as_is))
        def _():
            fill(row_ref[0, :, here].T, row_ref[1, :, here].T)

        return carry

    lax.fori_loop(0, blocks, build, 0)

    def source_tile(i, carry):
        rows = pl.ds(pl.multiple_of(i * TILE, TILE), TILE)
        field = (i * col_tiles + j) * 3
        lo, extent, taper = aperture[field], aperture[field + 1], aperture[field + 2]
        acc[...] = jnp.zeros_like(acc)
        position = lo + taper
        inner = extent - 2 * taper
        size = 1
        while size * 2 <= blocks:
            size *= 2
        while size:
            present = lax.rem(inner // size, 2)

            @pl.when(present == 1)
            def _(size=size, position=position):
                part = span(position, size)
                acc[...] += jnp.dot(
                    lhs[rows, part], rhs[part, :], preferred_element_type=jnp.float32
                )

            position = position + present * size
            size //= 2
        for width in (1, 2):

            @pl.when(taper == width)
            def _(width=width):
                total = acc[...]
                for p in range(width):
                    weight = np.float32(p + 1) / np.float32(width + 1)
                    for block in (lo + p, lo + extent - 1 - p):
                        part = span(block, 1)
                        scaled = (lhs[rows, part].astype(jnp.float32) * weight).astype(jnp.bfloat16)
                        total += jnp.dot(scaled, rhs[part, :], preferred_element_type=jnp.float32)
                acc[...] = total

        out_ref[0, rows, :] = acc[:, :TILE]
        out_ref[1, rows, :] = acc[:, TILE:]
        return carry

    lax.fori_loop(0, row_tiles, source_tile, 0)


def apply(aperture, straight, places, left, column, row, own_rows, own_cols):
    whole = column.shape[1]
    blocks = whole // TILE
    row_tiles, col_tiles = own_rows // TILE, own_cols // TILE
    mixed = row is not None
    in_specs = [
        pl.BlockSpec(
            (2, own_rows, whole), lambda j, f, h, p: (0, p[0], 0), pipeline_mode=pl.Buffered(1)
        ),
        pl.BlockSpec((2, whole, TILE), lambda j, f, h, p: (0, 0, p[1] + j)),
    ]
    operands = [left, column]
    if mixed:
        in_specs.append(pl.BlockSpec((2, TILE, whole), lambda j, f, h, p: (0, p[1] + j, 0)))
        operands.append(row)
    flops = 8 * own_rows * own_cols * whole
    return pl.pallas_call(
        functools.partial(apply_kernel, row_tiles, col_tiles, blocks, mixed),
        out_shape=jax.ShapeDtypeStruct((2, own_rows, own_cols), jnp.float32),
        grid_spec=pltpu.PrefetchScalarGridSpec(
            num_scalar_prefetch=3,
            grid=(col_tiles,),
            in_specs=in_specs,
            out_specs=pl.BlockSpec((2, own_rows, TILE), lambda j, f, h, p: (0, 0, j)),
            scratch_shapes=[
                pltpu.VMEM((own_rows, 2 * whole), jnp.bfloat16),
                pltpu.VMEM((2 * whole, 2 * TILE), jnp.bfloat16),
                pltpu.VMEM((TILE, 2 * TILE), jnp.float32),
            ],
        ),
        compiler_params=pltpu.CompilerParams(vmem_limit_bytes=58 * 1024 * 1024),
        cost_estimate=pl.CostEstimate(
            flops=flops, bytes_accessed=40 * own_rows * whole, transcendentals=0
        ),
        name="apply_apertures",
    )(aperture.reshape(-1), straight.reshape(-1), places, *operands)


def held_straight(s, strip, first_tile, col_tiles):
    a, b, d = s + 1 - 2 * (s % 2), (s + 2) % 4, 3 - s
    per_half = strip // TILE // 2
    q = (jnp.arange(8 * per_half, dtype=jnp.int32) // per_half)[:, None]
    j = ((first_tile + jnp.arange(col_tiles, dtype=jnp.int32)) // per_half)[None, :]
    u, u_half, t, t_half = q // 2, q % 2, j // 2, j % 2
    held = (u == s) | ((u == t) & (t != s)) | ((u == a) & (t == d)) | ((u == b) & (t == d))
    held = held | ((u == a) & (t == b) & (u_half == 0)) | ((u == b) & (t == a) & (t_half == 1))
    return held.astype(jnp.int32)


def shards(square, recorded, aperture):
    own_rows, own_cols = recorded.shape[2], recorded.shape[3]
    row_tiles, col_tiles = own_rows // TILE, own_cols // TILE
    if square:
        s = lax.axis_index("src").astype(jnp.int32)
        first_tile = lax.axis_index("rcv").astype(jnp.int32) * col_tiles
        whole = exchange(recorded)
        straight = held_straight(s, own_rows, first_tile, col_tiles)
        places = jnp.stack([s, first_tile])
        out = apply(aperture, straight, places, whole, whole, whole, own_rows, own_cols)
        return out[None]
    places = jnp.zeros((2,), jnp.int32)
    straight = jnp.ones((1,), jnp.int32)
    left = lax.all_gather(recorded, "rcv", axis=3, tiled=True)
    column = lax.all_gather(recorded, "src", axis=2, tiled=True)
    outs = [
        apply(aperture, straight, places, left[f], column[f], None, own_rows, own_cols)
        for f in range(recorded.shape[0])
    ]
    return jnp.stack(outs)


def solution(mesh):
    square = mesh.shape["src"] == 4 and mesh.shape["rcv"] == 2
    in_specs = (P("grp", None, "src", "rcv"), P(("grp", "src"), "rcv", None))
    out_specs = P("grp", None, "src", "rcv")
    return jax.shard_map(
        functools.partial(shards, square),
        mesh=mesh,
        in_specs=in_specs,
        out_specs=out_specs,
        check_vma=False,
    )
```

```python
import functools

import jax
import jax.numpy as jnp
import numpy as np
from jax import lax
from jax.experimental import pallas as pl
from jax.experimental.pallas import tpu as pltpu
from jax.sharding import PartitionSpec as P

TILE = 128
COPIES = 14


def fused_kernel(x_ref, w_ref, out_ref, g_ref, lhs, raw, rhs, send_sems, recv_sems, local_sem):
    strip = x_ref.shape[2]
    half = strip // 2
    tiles = strip // TILE
    depth = 2 * strip
    s = lax.axis_index("src")
    r = lax.axis_index("rcv")
    a = s + 1 - 2 * lax.rem(s, 2)
    b = lax.rem(s + 2, 4)
    d = 3 - s
    to_x, to_y, to_sibling = {"src": a}, {"src": b}, {"rcv": 1 - r}
    home = r == s // 2

    def place(u, t, rows=(0, strip), cols=(0, strip)):
        return g_ref.at[
            :,
            pl.ds(pl.multiple_of(u * strip + rows[0], half), rows[1]),
            pl.ds(pl.multiple_of(t * strip + cols[0], half), cols[1]),
        ]

    def own(t, rows=(0, strip), cols=(0, strip)):
        return x_ref.at[
            0,
            :,
            pl.ds(rows[0], rows[1]),
            pl.ds(pl.multiple_of(lax.rem(t, 2) * strip + cols[0], half), cols[1]),
        ]

    def copy(number, source, target, device):
        return pltpu.make_async_remote_copy(
            src_ref=source,
            dst_ref=target,
            send_sem=send_sems.at[number],
            recv_sem=recv_sems.at[number],
            device_id=device,
            device_id_type=pl.DeviceIdType.MESH,
        )

    def arrive(number, target, device):
        copy(number, target, target, device).wait_recv()

    def load(source, rows=(0, strip), cols=(0, strip)):
        target = raw.at[:, pl.ds(rows[0], rows[1]), pl.ds(cols[0], cols[1])]
        fetch = pltpu.make_async_copy(source, target, local_sem)
        fetch.start()
        fetch.wait()

    def fill_left(u):
        def one(k, carry):
            for c in range(2):
                lane = pl.multiple_of(u * depth + (2 * k + c) * TILE, TILE)
                lhs[:, pl.ds(lane, TILE)] = raw[
                    c, :strip, pl.ds(pl.multiple_of(k * TILE, TILE), TILE)
                ]
            return carry

        lax.fori_loop(0, tiles, one, 0)

    def at(tile, offset=0):
        return pl.ds(pl.multiple_of(tile * TILE + offset, TILE), TILE)

    def build(j, low, high, flip, offset):
        def one(k, carry):
            row, col = (j, k) if flip else (k, j)
            real = raw[0, at(row, offset), at(col)]
            imag = raw[1, at(row, offset), at(col)]
            if flip:
                real, imag = real.T, imag.T
            first, second = at(2 * k), at(2 * k + 1)
            rhs[first, :TILE] = real
            rhs[first, TILE:] = imag
            rhs[second, :TILE] = -imag
            rhs[second, TILE:] = real
            return carry

        lax.fori_loop(low, high, one, 0)

    def multiply(u, t, mode, first):
        left = pl.ds(pl.multiple_of(u * depth, depth), depth)
        group = 2 * TILE if tiles % 2 == 0 else TILE
        side = lax.rem(t, 2)

        def column(j, carry):
            if mode == "mixed home":

                @pl.when(j < tiles // 2)
                def _():
                    build(j, 0, tiles, True, 0)

                @pl.when(j >= tiles // 2)
                def _():
                    build(j, 0, tiles, False, half)

            elif mode == "mixed other":
                build(j, 0, tiles // 2, False, 0)
                build(j, tiles // 2, tiles, True, half)
            else:
                build(j, 0, tiles, mode == "flip", 0)
            lanes = at(side * tiles + j)

            def source(i, carry):
                rows = pl.ds(pl.multiple_of(i * group, group), group)
                parts = []
                for n in range(group // TILE):
                    tile = i * (group // TILE) + n
                    weight = w_ref[pl.ds(tile * 2 * tiles + side * tiles + j, 1), left]
                    piece = lhs[pl.ds(pl.multiple_of(tile * TILE, TILE), TILE), left]
                    parts.append((piece.astype(jnp.float32) * weight).astype(jnp.bfloat16))
                scaled = jnp.concatenate(parts, axis=0)
                product = jnp.dot(scaled, rhs[...], preferred_element_type=jnp.float32)
                if first:
                    out_ref[0, rows, lanes] = product[:, :TILE]
                    out_ref[1, rows, lanes] = product[:, TILE:]
                else:
                    out_ref[0, rows, lanes] += product[:, :TILE]
                    out_ref[1, rows, lanes] += product[:, TILE:]
                return carry

            lax.fori_loop(0, strip // group, source, 0)
            return carry

        lax.fori_loop(0, tiles, column, 0)

    def own_place(core):
        return g_ref.at[
            :,
            pl.ds(pl.multiple_of(s * strip, strip), strip),
            pl.ds(pl.multiple_of(core * 2 * strip, strip), 2 * strip),
        ]

    def load_mixed():
        load(place(a, b, lower), rows=(0, half))
        load(place(b, a, cols=upper), rows=(half, strip), cols=upper)

    lower, upper = (0, half), (half, half)
    barrier = pltpu.get_barrier_semaphore()
    for device in (to_x, to_y, to_sibling):
        pl.semaphore_signal(barrier, inc=1, device_id=device, device_id_type=pl.DeviceIdType.MESH)
    pl.semaphore_wait(barrier, 3)

    @pl.when(home)
    def _():
        sends = [
            copy(0, x_ref.at[0], own_place(r), to_sibling),
            copy(1, own(s, upper), place(s, s, upper), to_x),
            copy(3, own(s, lower), place(s, s, lower), to_y),
            copy(2, own(s, lower), place(s, s, lower), to_x),
            copy(4, own(s, upper), place(s, s, upper), to_y),
            copy(5, own(a), place(s, a), to_y),
        ]
        for send in sends:
            send.start()
        load(own(s))
        fill_left(s)
        multiply(s, s, "as is", True)
        load(own(a))
        fill_left(a)
        multiply(s, a, "as is", True)
        arrive(1, place(a, a, upper), to_x)
        forward = copy(6, place(a, a, upper), place(a, a, upper), to_y)
        forward.start()
        multiply(a, s, "flip", False)
        arrive(0, own_place(1 - r), to_sibling)
        load(place(s, b))
        fill_left(b)
        multiply(b, s, "flip", False)
        arrive(9, place(b, a, cols=upper), to_y)
        share = copy(11, place(b, a, cols=upper), place(b, a, cols=upper), to_sibling)
        share.start()
        load(place(s, d))
        fill_left(d)
        multiply(d, s, "flip", False)
        arrive(2, place(a, a, lower), to_x)
        load(place(a, a))
        multiply(a, a, "as is", False)
        arrive(12, place(a, d), to_sibling)
        load(place(a, d))
        multiply(d, a, "flip", False)
        arrive(13, place(a, b, lower), to_sibling)
        load_mixed()
        multiply(b, a, "mixed home", False)
        for send in sends + [forward, share]:
            send.wait_send()

    @pl.when(jnp.logical_not(home))
    def _():
        sends = [
            copy(0, x_ref.at[0], own_place(r), to_sibling),
            copy(9, own(d, cols=upper), place(s, d, cols=upper), to_y),
            copy(7, own(b), place(s, b), to_x),
            copy(8, own(d, lower), place(s, d, lower), to_x),
        ]
        for send in sends:
            send.start()
        arrive(0, own_place(1 - r), to_sibling)
        load(place(s, a))
        fill_left(a)
        load(place(s, s))
        fill_left(s)
        arrive(3, place(b, b, lower), to_y)
        forward = copy(10, place(b, b, lower), place(b, b, lower), to_x)
        forward.start()
        load(own(b))
        fill_left(b)
        multiply(s, b, "as is", True)
        load(own(d))
        fill_left(d)
        multiply(s, d, "as is", True)
        arrive(4, place(b, b, upper), to_y)
        load(place(b, b))
        multiply(b, b, "as is", False)
        arrive(7, place(a, d), to_x)
        share = copy(12, place(a, d), place(a, d), to_sibling)
        share.start()
        load(place(a, d))
        multiply(a, d, "as is", False)
        arrive(8, place(a, b, lower), to_x)
        share_half = copy(13, place(a, b, lower), place(a, b, lower), to_sibling)
        share_half.start()
        arrive(11, place(b, a, cols=upper), to_sibling)
        load_mixed()
        multiply(a, b, "mixed other", False)
        arrive(5, place(b, d), to_y)
        load(place(b, d))
        multiply(b, d, "as is", False)
        multiply(d, b, "flip", False)
        arrive(6, place(d, d, upper), to_y)
        arrive(10, place(d, d, lower), to_x)
        load(place(d, d))
        multiply(d, d, "as is", False)
        for send in sends + [forward, share, share_half]:
            send.wait_send()


def fused(recorded, weights):
    rows, cols = recorded.shape[2], recorded.shape[3]
    whole = 4 * rows
    out, _ = pl.pallas_call(
        fused_kernel,
        out_shape=(
            jax.ShapeDtypeStruct((2, rows, cols), jnp.float32),
            jax.ShapeDtypeStruct((2, whole, whole), recorded.dtype),
        ),
        in_specs=[pl.BlockSpec(memory_space=pl.ANY), pl.BlockSpec(memory_space=pltpu.VMEM)],
        out_specs=(pl.BlockSpec(memory_space=pltpu.VMEM), pl.BlockSpec(memory_space=pl.ANY)),
        scratch_shapes=[
            pltpu.VMEM((rows, 2 * whole), jnp.bfloat16),
            pltpu.VMEM((2, rows + rows // 2, rows), jnp.bfloat16),
            pltpu.VMEM((2 * rows, 2 * TILE), jnp.bfloat16),
            pltpu.SemaphoreType.DMA((COPIES,)),
            pltpu.SemaphoreType.DMA((COPIES,)),
            pltpu.SemaphoreType.DMA,
        ],
        compiler_params=pltpu.CompilerParams(
            collective_id=0, has_side_effects=True, vmem_limit_bytes=60 * 1024 * 1024
        ),
        cost_estimate=pl.CostEstimate(
            flops=8 * rows * cols * whole, bytes_accessed=40 * rows * whole, transcendentals=0
        ),
        name="exchange_and_multiply",
    )(recorded, weights)
    return out


def tile_weights(aperture, blocks):
    offset = jnp.arange(blocks, dtype=jnp.int32)[None, None, :] - aperture[..., 0:1]
    extent = aperture[..., 1:2]
    margin = jnp.minimum(offset, extent - 1 - offset)
    ramp = (margin + 1).astype(jnp.float32) / (aperture[..., 2:3] + 1).astype(jnp.float32)
    return jnp.where((offset >= 0) & (offset < extent), jnp.minimum(1.0, ramp), 0.0)


def apply_kernel(
    row_tiles, col_tiles, blocks, mixed, aperture, straight, places, left_ref, *refs
):
    if mixed:
        column_ref, row_ref, out_ref, lhs, rhs, acc = refs
    else:
        column_ref, out_ref, lhs, rhs, acc = refs
    j = pl.program_id(0)

    def span(block, count):
        return pl.ds(pl.multiple_of(block * (2 * TILE), 2 * TILE), count * 2 * TILE)

    @pl.when(j == 0)
    def _():
        def interleave(k, carry):
            for c in range(2):
                lhs[:, pl.ds(pl.multiple_of((2 * k + c) * TILE, TILE), TILE)] = left_ref[
                    c, :, pl.ds(pl.multiple_of(k * TILE, TILE), TILE)
                ]
            return carry

        lax.fori_loop(0, blocks, interleave, 0)

    def build(k, carry):
        here = pl.ds(pl.multiple_of(k * TILE, TILE), TILE)
        first = pl.ds(pl.multiple_of(k * 2 * TILE, TILE), TILE)
        second = pl.ds(pl.multiple_of(k * 2 * TILE + TILE, TILE), TILE)

        def fill(real, imag):
            rhs[first, :TILE] = real
            rhs[first, TILE:] = imag
            rhs[second, :TILE] = -imag
            rhs[second, TILE:] = real

        if not mixed:
            fill(column_ref[0, here, :], column_ref[1, here, :])
            return carry
        as_is = straight[k * col_tiles + j] == 1

        @pl.when(as_is)
        def _():
            fill(column_ref[0, here, :], column_ref[1, here, :])

        @pl.when(jnp.logical_not(as_is))
        def _():
            fill(row_ref[0, :, here].T, row_ref[1, :, here].T)

        return carry

    lax.fori_loop(0, blocks, build, 0)

    def source_tile(i, carry):
        rows = pl.ds(pl.multiple_of(i * TILE, TILE), TILE)
        field = (i * col_tiles + j) * 3
        lo, extent, taper = aperture[field], aperture[field + 1], aperture[field + 2]
        acc[...] = jnp.zeros_like(acc)
        position = lo + taper
        inner = extent - 2 * taper
        size = 1
        while size * 2 <= blocks:
            size *= 2
        while size:
            present = lax.rem(inner // size, 2)

            @pl.when(present == 1)
            def _(size=size, position=position):
                part = span(position, size)
                acc[...] += jnp.dot(
                    lhs[rows, part], rhs[part, :], preferred_element_type=jnp.float32
                )

            position = position + present * size
            size //= 2
        for width in (1, 2):

            @pl.when(taper == width)
            def _(width=width):
                total = acc[...]
                for p in range(width):
                    weight = np.float32(p + 1) / np.float32(width + 1)
                    for block in (lo + p, lo + extent - 1 - p):
                        part = span(block, 1)
                        scaled = (lhs[rows, part].astype(jnp.float32) * weight).astype(jnp.bfloat16)
                        total += jnp.dot(scaled, rhs[part, :], preferred_element_type=jnp.float32)
                acc[...] = total

        out_ref[0, rows, :] = acc[:, :TILE]
        out_ref[1, rows, :] = acc[:, TILE:]
        return carry

    lax.fori_loop(0, row_tiles, source_tile, 0)


def apply(aperture, straight, places, left, column, row, own_rows, own_cols):
    whole = column.shape[1]
    blocks = whole // TILE
    row_tiles, col_tiles = own_rows // TILE, own_cols // TILE
    mixed = row is not None
    in_specs = [
        pl.BlockSpec(
            (2, own_rows, whole), lambda j, f, h, p: (0, p[0], 0), pipeline_mode=pl.Buffered(1)
        ),
        pl.BlockSpec((2, whole, TILE), lambda j, f, h, p: (0, 0, p[1] + j)),
    ]
    operands = [left, column]
    if mixed:
        in_specs.append(pl.BlockSpec((2, TILE, whole), lambda j, f, h, p: (0, p[1] + j, 0)))
        operands.append(row)
    flops = 8 * own_rows * own_cols * whole
    return pl.pallas_call(
        functools.partial(apply_kernel, row_tiles, col_tiles, blocks, mixed),
        out_shape=jax.ShapeDtypeStruct((2, own_rows, own_cols), jnp.float32),
        grid_spec=pltpu.PrefetchScalarGridSpec(
            num_scalar_prefetch=3,
            grid=(col_tiles,),
            in_specs=in_specs,
            out_specs=pl.BlockSpec((2, own_rows, TILE), lambda j, f, h, p: (0, 0, j)),
            scratch_shapes=[
                pltpu.VMEM((own_rows, 2 * whole), jnp.bfloat16),
                pltpu.VMEM((2 * whole, 2 * TILE), jnp.bfloat16),
                pltpu.VMEM((TILE, 2 * TILE), jnp.float32),
            ],
        ),
        compiler_params=pltpu.CompilerParams(vmem_limit_bytes=58 * 1024 * 1024),
        cost_estimate=pl.CostEstimate(
            flops=flops, bytes_accessed=40 * own_rows * whole, transcendentals=0
        ),
        name="apply_apertures",
    )(aperture.reshape(-1), straight.reshape(-1), places, *operands)


def shards(square, recorded, aperture):
    own_rows, own_cols = recorded.shape[2], recorded.shape[3]
    row_tiles, col_tiles = own_rows // TILE, own_cols // TILE
    if square:
        weights = tile_weights(aperture, 4 * row_tiles)
        weights = jnp.repeat(weights.reshape(row_tiles * col_tiles, -1), 2 * TILE, axis=1)
        out = fused(recorded, weights)
        return out[None]
    places = jnp.zeros((2,), jnp.int32)
    straight = jnp.ones((1,), jnp.int32)
    left = lax.all_gather(recorded, "rcv", axis=3, tiled=True)
    column = lax.all_gather(recorded, "src", axis=2, tiled=True)
    outs = [
        apply(aperture, straight, places, left[f], column[f], None, own_rows, own_cols)
        for f in range(recorded.shape[0])
    ]
    return jnp.stack(outs)


def solution(mesh):
    square = mesh.shape["src"] == 4 and mesh.shape["rcv"] == 2
    in_specs = (P("grp", None, "src", "rcv"), P(("grp", "src"), "rcv", None))
    out_specs = P("grp", None, "src", "rcv")
    return jax.shard_map(
        functools.partial(shards, square),
        mesh=mesh,
        in_specs=in_specs,
        out_specs=out_specs,
        check_vma=False,
    )
```

```python
import functools

import jax
import jax.numpy as jnp
import numpy as np
from jax import lax
from jax.experimental import pallas as pl
from jax.experimental.pallas import tpu as pltpu
from jax.sharding import PartitionSpec as P

TILE = 128
COPIES = 26


def fused_kernel(x_ref, w_ref, out_ref, g_ref, lhs, raw, rhs, send_sems, recv_sems, local_sem):
    strip = x_ref.shape[2]
    half, band = strip // 2, strip // 4
    tiles = strip // TILE
    depth = 2 * strip
    s = lax.axis_index("src")
    r = lax.axis_index("rcv")
    a = s + 1 - 2 * lax.rem(s, 2)
    b = lax.rem(s + 2, 4)
    d = 3 - s
    to_x, to_y, to_sibling = {"src": a}, {"src": b}, {"rcv": 1 - r}
    home = r == s // 2

    def place(u, t, rows=(0, strip), cols=(0, strip)):
        return g_ref.at[
            :,
            pl.ds(pl.multiple_of(u * strip + rows[0], TILE), rows[1]),
            pl.ds(pl.multiple_of(t * strip + cols[0], TILE), cols[1]),
        ]

    def own(t, rows=(0, strip), cols=(0, strip)):
        return x_ref.at[
            0,
            :,
            pl.ds(rows[0], rows[1]),
            pl.ds(pl.multiple_of(lax.rem(t, 2) * strip + cols[0], TILE), cols[1]),
        ]

    def copy(number, source, target, device):
        return pltpu.make_async_remote_copy(
            src_ref=source,
            dst_ref=target,
            send_sem=send_sems.at[number],
            recv_sem=recv_sems.at[number],
            device_id=device,
            device_id_type=pl.DeviceIdType.MESH,
        )

    def arrive(number, target, device):
        copy(number, target, target, device).wait_recv()

    def load(source, rows=(0, strip), cols=(0, strip)):
        target = raw.at[:, pl.ds(rows[0], rows[1]), pl.ds(cols[0], cols[1])]
        fetch = pltpu.make_async_copy(source, target, local_sem)
        fetch.start()
        fetch.wait()

    def fill_left(u):
        def one(k, carry):
            for c in range(2):
                lane = pl.multiple_of(u * depth + (2 * k + c) * TILE, TILE)
                lhs[:, pl.ds(lane, TILE)] = raw[
                    c, :strip, pl.ds(pl.multiple_of(k * TILE, TILE), TILE)
                ]
            return carry

        lax.fori_loop(0, tiles, one, 0)

    def at(tile, offset=0):
        return pl.ds(pl.multiple_of(tile * TILE + offset, TILE), TILE)

    def build(j, low, high, flip, offset):
        def one(k, carry):
            row, col = (j, k) if flip else (k, j)
            real = raw[0, at(row, offset), at(col)]
            imag = raw[1, at(row, offset), at(col)]
            if flip:
                real, imag = real.T, imag.T
            first, second = at(2 * k), at(2 * k + 1)
            rhs[first, :TILE] = real
            rhs[first, TILE:] = imag
            rhs[second, :TILE] = -imag
            rhs[second, TILE:] = real
            return carry

        lax.fori_loop(low, high, one, 0)

    def multiply(u, t, mode, first):
        group = 2 * TILE if tiles % 2 == 0 else TILE
        side = lax.rem(t, 2)

        def column(j, carry):
            if mode == "mixed home":

                @pl.when(j < tiles // 2)
                def _():
                    build(j, 0, tiles, True, 0)

                @pl.when(j >= tiles // 2)
                def _():
                    build(j, 0, tiles, False, half)

            elif mode == "mixed other":
                build(j, 0, tiles // 2, False, 0)
                build(j, tiles // 2, tiles, True, half)
            elif mode == "diagonal":
                stair = (j // (tiles // 4) + 1) * (tiles // 4)
                build(j, 0, stair, False, 0)
                build(j, stair, tiles, True, 0)
            else:
                build(j, 0, tiles, mode == "flip", 0)
            lanes = at(side * tiles + j)

            def source(i, carry):
                rows = pl.ds(pl.multiple_of(i * group, group), group)
                parts = []
                for n in range(group // TILE):
                    tile = i * (group // TILE) + n
                    first_weight = ((tile * 2 + side) * tiles + j) * 4 * tiles + u * tiles
                    blocks = []
                    for k in range(tiles):
                        lane = pl.multiple_of(u * depth + k * 2 * TILE, 2 * TILE)
                        piece = lhs[pl.ds(pl.multiple_of(tile * TILE, TILE), TILE), pl.ds(lane, 2 * TILE)]
                        weight = w_ref[first_weight + k]
                        blocks.append((piece.astype(jnp.float32) * weight).astype(jnp.bfloat16))
                    parts.append(jnp.concatenate(blocks, axis=1))
                scaled = jnp.concatenate(parts, axis=0)
                product = jnp.dot(scaled, rhs[...], preferred_element_type=jnp.float32)
                if first:
                    out_ref[0, rows, lanes] = product[:, :TILE]
                    out_ref[1, rows, lanes] = product[:, TILE:]
                else:
                    out_ref[0, rows, lanes] += product[:, :TILE]
                    out_ref[1, rows, lanes] += product[:, TILE:]
                return carry

            lax.fori_loop(0, strip // group, source, 0)
            return carry

        lax.fori_loop(0, tiles, column, 0)

    def stair(u, i):
        return place(u, u, (i * band, band), (i * band, strip - i * band))

    def own_stair(i):
        return own(s, (i * band, band), (i * band, strip - i * band))

    def load_diagonal(u):
        for i in range(4):
            load(stair(u, i), (i * band, band), (i * band, strip - i * band))

    def own_place(core):
        return g_ref.at[
            :,
            pl.ds(pl.multiple_of(s * strip, strip), strip),
            pl.ds(pl.multiple_of(core * 2 * strip, strip), 2 * strip),
        ]

    def load_mixed():
        load(place(a, b, lower), rows=(0, half))
        load(place(b, a, cols=upper), rows=(half, strip), cols=upper)

    lower, upper = (0, half), (half, half)
    barrier = pltpu.get_barrier_semaphore()
    for device in (to_x, to_y, to_sibling):
        pl.semaphore_signal(barrier, inc=1, device_id=device, device_id_type=pl.DeviceIdType.MESH)
    pl.semaphore_wait(barrier, 3)

    @pl.when(home)
    def _():
        sends = [
            copy(0, x_ref.at[0], own_place(r), to_sibling),
            copy(15, own_stair(1), stair(s, 1), to_x),
            copy(18, own_stair(0), stair(s, 0), to_y),
            copy(16, own_stair(2), stair(s, 2), to_x),
            copy(21, own_stair(3), stair(s, 3), to_y),
            copy(14, own_stair(0), stair(s, 0), to_x),
            copy(19, own_stair(1), stair(s, 1), to_y),
            copy(17, own_stair(3), stair(s, 3), to_x),
            copy(20, own_stair(2), stair(s, 2), to_y),
            copy(5, own(a), place(s, a), to_y),
        ]
        for send in sends:
            send.start()
        load(own(s))
        fill_left(s)
        multiply(s, s, "as is", True)
        load(own(a))
        fill_left(a)
        multiply(s, a, "as is", True)
        forwards = []
        for i in (1, 2):
            arrive(14 + i, stair(a, i), to_x)
            forwards.append(copy(21 + i, stair(a, i), stair(a, i), to_y))
            forwards[-1].start()
        multiply(a, s, "flip", False)
        arrive(0, own_place(1 - r), to_sibling)
        load(place(s, b))
        fill_left(b)
        multiply(b, s, "flip", False)
        arrive(9, place(b, a, cols=upper), to_y)
        share = copy(11, place(b, a, cols=upper), place(b, a, cols=upper), to_sibling)
        share.start()
        load(place(s, d))
        fill_left(d)
        multiply(d, s, "flip", False)
        arrive(14, stair(a, 0), to_x)
        arrive(17, stair(a, 3), to_x)
        load_diagonal(a)
        multiply(a, a, "diagonal", False)
        arrive(12, place(a, d), to_sibling)
        load(place(a, d))
        multiply(d, a, "flip", False)
        arrive(13, place(a, b, lower), to_sibling)
        load_mixed()
        multiply(b, a, "mixed home", False)
        for send in sends + forwards + [share]:
            send.wait_send()

    @pl.when(jnp.logical_not(home))
    def _():
        sends = [
            copy(0, x_ref.at[0], own_place(r), to_sibling),
            copy(9, own(d, cols=upper), place(s, d, cols=upper), to_y),
            copy(7, own(b), place(s, b), to_x),
            copy(8, own(d, lower), place(s, d, lower), to_x),
        ]
        for send in sends:
            send.start()
        arrive(0, own_place(1 - r), to_sibling)
        load(place(s, a))
        fill_left(a)
        load(place(s, s))
        fill_left(s)
        forwards = []
        for n, i in enumerate((0, 3)):
            arrive(18 + i, stair(b, i), to_y)
            forwards.append(copy(24 + n, stair(b, i), stair(b, i), to_x))
            forwards[-1].start()
        load(own(b))
        fill_left(b)
        multiply(s, b, "as is", True)
        load(own(d))
        fill_left(d)
        multiply(s, d, "as is", True)
        arrive(19, stair(b, 1), to_y)
        arrive(20, stair(b, 2), to_y)
        load_diagonal(b)
        multiply(b, b, "diagonal", False)
        arrive(7, place(a, d), to_x)
        share = copy(12, place(a, d), place(a, d), to_sibling)
        share.start()
        load(place(a, d))
        multiply(a, d, "as is", False)
        arrive(8, place(a, b, lower), to_x)
        share_half = copy(13, place(a, b, lower), place(a, b, lower), to_sibling)
        share_half.start()
        arrive(11, place(b, a, cols=upper), to_sibling)
        load_mixed()
        multiply(a, b, "mixed other", False)
        arrive(5, place(b, d), to_y)
        load(place(b, d))
        multiply(b, d, "as is", False)
        multiply(d, b, "flip", False)
        arrive(22, stair(d, 1), to_y)
        arrive(23, stair(d, 2), to_y)
        arrive(24, stair(d, 0), to_x)
        arrive(25, stair(d, 3), to_x)
        load_diagonal(d)
        multiply(d, d, "diagonal", False)
        for send in sends + forwards + [share, share_half]:
            send.wait_send()


def fused(recorded, weights):
    rows, cols = recorded.shape[2], recorded.shape[3]
    whole = 4 * rows
    out, _ = pl.pallas_call(
        fused_kernel,
        out_shape=(
            jax.ShapeDtypeStruct((2, rows, cols), jnp.float32),
            jax.ShapeDtypeStruct((2, whole, whole), recorded.dtype),
        ),
        in_specs=[pl.BlockSpec(memory_space=pl.ANY), pl.BlockSpec(memory_space=pltpu.SMEM)],
        out_specs=(pl.BlockSpec(memory_space=pltpu.VMEM), pl.BlockSpec(memory_space=pl.ANY)),
        scratch_shapes=[
            pltpu.VMEM((rows, 2 * whole), jnp.bfloat16),
            pltpu.VMEM((2, rows + rows // 2, rows), jnp.bfloat16),
            pltpu.VMEM((2 * rows, 2 * TILE), jnp.bfloat16),
            pltpu.SemaphoreType.DMA((COPIES,)),
            pltpu.SemaphoreType.DMA((COPIES,)),
            pltpu.SemaphoreType.DMA,
        ],
        compiler_params=pltpu.CompilerParams(
            collective_id=0, has_side_effects=True, vmem_limit_bytes=60 * 1024 * 1024
        ),
        cost_estimate=pl.CostEstimate(
            flops=8 * rows * cols * whole, bytes_accessed=40 * rows * whole, transcendentals=0
        ),
        name="exchange_and_multiply",
    )(recorded, weights)
    return out


def tile_weights(aperture, blocks):
    offset = jnp.arange(blocks, dtype=jnp.int32)[None, None, :] - aperture[..., 0:1]
    extent = aperture[..., 1:2]
    margin = jnp.minimum(offset, extent - 1 - offset)
    ramp = (margin + 1).astype(jnp.float32) / (aperture[..., 2:3] + 1).astype(jnp.float32)
    return jnp.where((offset >= 0) & (offset < extent), jnp.minimum(1.0, ramp), 0.0)


def apply_kernel(
    row_tiles, col_tiles, blocks, mixed, aperture, straight, places, left_ref, *refs
):
    if mixed:
        column_ref, row_ref, out_ref, lhs, rhs, acc = refs
    else:
        column_ref, out_ref, lhs, rhs, acc = refs
    j = pl.program_id(0)

    def span(block, count):
        return pl.ds(pl.multiple_of(block * (2 * TILE), 2 * TILE), count * 2 * TILE)

    @pl.when(j == 0)
    def _():
        def interleave(k, carry):
            for c in range(2):
                lhs[:, pl.ds(pl.multiple_of((2 * k + c) * TILE, TILE), TILE)] = left_ref[
                    c, :, pl.ds(pl.multiple_of(k * TILE, TILE), TILE)
                ]
            return carry

        lax.fori_loop(0, blocks, interleave, 0)

    def build(k, carry):
        here = pl.ds(pl.multiple_of(k * TILE, TILE), TILE)
        first = pl.ds(pl.multiple_of(k * 2 * TILE, TILE), TILE)
        second = pl.ds(pl.multiple_of(k * 2 * TILE + TILE, TILE), TILE)

        def fill(real, imag):
            rhs[first, :TILE] = real
            rhs[first, TILE:] = imag
            rhs[second, :TILE] = -imag
            rhs[second, TILE:] = real

        if not mixed:
            fill(column_ref[0, here, :], column_ref[1, here, :])
            return carry
        as_is = straight[k * col_tiles + j] == 1

        @pl.when(as_is)
        def _():
            fill(column_ref[0, here, :], column_ref[1, here, :])

        @pl.when(jnp.logical_not(as_is))
        def _():
            fill(row_ref[0, :, here].T, row_ref[1, :, here].T)

        return carry

    lax.fori_loop(0, blocks, build, 0)

    def source_tile(i, carry):
        rows = pl.ds(pl.multiple_of(i * TILE, TILE), TILE)
        field = (i * col_tiles + j) * 3
        lo, extent, taper = aperture[field], aperture[field + 1], aperture[field + 2]
        acc[...] = jnp.zeros_like(acc)
        position = lo + taper
        inner = extent - 2 * taper
        size = 1
        while size * 2 <= blocks:
            size *= 2
        while size:
            present = lax.rem(inner // size, 2)

            @pl.when(present == 1)
            def _(size=size, position=position):
                part = span(position, size)
                acc[...] += jnp.dot(
                    lhs[rows, part], rhs[part, :], preferred_element_type=jnp.float32
                )

            position = position + present * size
            size //= 2
        for width in (1, 2):

            @pl.when(taper == width)
            def _(width=width):
                total = acc[...]
                for p in range(width):
                    weight = np.float32(p + 1) / np.float32(width + 1)
                    for block in (lo + p, lo + extent - 1 - p):
                        part = span(block, 1)
                        scaled = (lhs[rows, part].astype(jnp.float32) * weight).astype(jnp.bfloat16)
                        total += jnp.dot(scaled, rhs[part, :], preferred_element_type=jnp.float32)
                acc[...] = total

        out_ref[0, rows, :] = acc[:, :TILE]
        out_ref[1, rows, :] = acc[:, TILE:]
        return carry

    lax.fori_loop(0, row_tiles, source_tile, 0)


def apply(aperture, straight, places, left, column, row, own_rows, own_cols):
    whole = column.shape[1]
    blocks = whole // TILE
    row_tiles, col_tiles = own_rows // TILE, own_cols // TILE
    mixed = row is not None
    in_specs = [
        pl.BlockSpec(
            (2, own_rows, whole), lambda j, f, h, p: (0, p[0], 0), pipeline_mode=pl.Buffered(1)
        ),
        pl.BlockSpec((2, whole, TILE), lambda j, f, h, p: (0, 0, p[1] + j)),
    ]
    operands = [left, column]
    if mixed:
        in_specs.append(pl.BlockSpec((2, TILE, whole), lambda j, f, h, p: (0, p[1] + j, 0)))
        operands.append(row)
    flops = 8 * own_rows * own_cols * whole
    return pl.pallas_call(
        functools.partial(apply_kernel, row_tiles, col_tiles, blocks, mixed),
        out_shape=jax.ShapeDtypeStruct((2, own_rows, own_cols), jnp.float32),
        grid_spec=pltpu.PrefetchScalarGridSpec(
            num_scalar_prefetch=3,
            grid=(col_tiles,),
            in_specs=in_specs,
            out_specs=pl.BlockSpec((2, own_rows, TILE), lambda j, f, h, p: (0, 0, j)),
            scratch_shapes=[
                pltpu.VMEM((own_rows, 2 * whole), jnp.bfloat16),
                pltpu.VMEM((2 * whole, 2 * TILE), jnp.bfloat16),
                pltpu.VMEM((TILE, 2 * TILE), jnp.float32),
            ],
        ),
        compiler_params=pltpu.CompilerParams(vmem_limit_bytes=58 * 1024 * 1024),
        cost_estimate=pl.CostEstimate(
            flops=flops, bytes_accessed=40 * own_rows * whole, transcendentals=0
        ),
        name="apply_apertures",
    )(aperture.reshape(-1), straight.reshape(-1), places, *operands)


def shards(square, recorded, aperture):
    own_rows, own_cols = recorded.shape[2], recorded.shape[3]
    row_tiles, col_tiles = own_rows // TILE, own_cols // TILE
    if square:
        weights = tile_weights(aperture, 4 * row_tiles)
        out = fused(recorded, weights.reshape(-1))
        return out[None]
    places = jnp.zeros((2,), jnp.int32)
    straight = jnp.ones((1,), jnp.int32)
    left = lax.all_gather(recorded, "rcv", axis=3, tiled=True)
    column = lax.all_gather(recorded, "src", axis=2, tiled=True)
    outs = [
        apply(aperture, straight, places, left[f], column[f], None, own_rows, own_cols)
        for f in range(recorded.shape[0])
    ]
    return jnp.stack(outs)


def solution(mesh):
    square = mesh.shape["src"] == 4 and mesh.shape["rcv"] == 2
    in_specs = (P("grp", None, "src", "rcv"), P(("grp", "src"), "rcv", None))
    out_specs = P("grp", None, "src", "rcv")
    return jax.shard_map(
        functools.partial(shards, square),
        mesh=mesh,
        in_specs=in_specs,
        out_specs=out_specs,
        check_vma=False,
    )
```

```python
import functools

import jax
import jax.numpy as jnp
import numpy as np
from jax import lax
from jax.experimental import pallas as pl
from jax.experimental.pallas import tpu as pltpu
from jax.sharding import PartitionSpec as P

TILE = 128
COPIES = 26


def fused_kernel(x_ref, w_ref, out_ref, g_ref, lhs, raw, rhs, send_sems, recv_sems, local_sem):
    strip = x_ref.shape[2]
    half, band = strip // 2, strip // 4
    tiles = strip // TILE
    depth = 2 * strip
    s = lax.axis_index("src")
    r = lax.axis_index("rcv")
    a = s + 1 - 2 * lax.rem(s, 2)
    b = lax.rem(s + 2, 4)
    d = 3 - s
    to_x, to_y, to_sibling = {"src": a}, {"src": b}, {"rcv": 1 - r}
    home = r == s // 2

    def place(u, t, rows=(0, strip), cols=(0, strip)):
        return g_ref.at[
            :,
            pl.ds(pl.multiple_of(u * strip + rows[0], TILE), rows[1]),
            pl.ds(pl.multiple_of(t * strip + cols[0], TILE), cols[1]),
        ]

    def own(t, rows=(0, strip), cols=(0, strip)):
        return x_ref.at[
            0,
            :,
            pl.ds(rows[0], rows[1]),
            pl.ds(pl.multiple_of(lax.rem(t, 2) * strip + cols[0], TILE), cols[1]),
        ]

    def copy(number, source, target, device):
        return pltpu.make_async_remote_copy(
            src_ref=source,
            dst_ref=target,
            send_sem=send_sems.at[number],
            recv_sem=recv_sems.at[number],
            device_id=device,
            device_id_type=pl.DeviceIdType.MESH,
        )

    def arrive(number, target, device):
        copy(number, target, target, device).wait_recv()

    def load(source, rows=(0, strip), cols=(0, strip)):
        target = raw.at[:, pl.ds(rows[0], rows[1]), pl.ds(cols[0], cols[1])]
        fetch = pltpu.make_async_copy(source, target, local_sem)
        fetch.start()
        fetch.wait()

    def fill_left(u):
        def one(k, carry):
            for c in range(2):
                lane = pl.multiple_of(u * depth + (2 * k + c) * TILE, TILE)
                lhs[:, pl.ds(lane, TILE)] = raw[
                    c, :strip, pl.ds(pl.multiple_of(k * TILE, TILE), TILE)
                ]
            return carry

        lax.fori_loop(0, tiles, one, 0)

    def at(tile, offset=0):
        return pl.ds(pl.multiple_of(tile * TILE + offset, TILE), TILE)

    def build(j, low, high, flip, offset):
        def one(k, carry):
            row, col = (j, k) if flip else (k, j)
            real = raw[0, at(row, offset), at(col)]
            imag = raw[1, at(row, offset), at(col)]
            if flip:
                real, imag = real.T, imag.T
            first, second = at(2 * k), at(2 * k + 1)
            rhs[first, :TILE] = real
            rhs[first, TILE:] = imag
            rhs[second, :TILE] = -imag
            rhs[second, TILE:] = real
            return carry

        static = isinstance(low, int) and isinstance(high, int)
        lax.fori_loop(low, high, one, 0, unroll=4 if static and (high - low) % 4 == 0 else 1)

    def multiply(u, t, mode, first):
        group = 4 * TILE if tiles % 4 == 0 else TILE
        side = lax.rem(t, 2)

        def column(j, carry):
            if mode == "mixed home":

                @pl.when(j < tiles // 2)
                def _():
                    build(j, 0, tiles, True, 0)

                @pl.when(j >= tiles // 2)
                def _():
                    build(j, 0, tiles, False, half)

            elif mode == "mixed other":
                build(j, 0, tiles // 2, False, 0)
                build(j, tiles // 2, tiles, True, half)
            elif mode == "diagonal":
                stair = (j // (tiles // 4) + 1) * (tiles // 4)
                build(j, 0, stair, False, 0)
                build(j, stair, tiles, True, 0)
            else:
                build(j, 0, tiles, mode == "flip", 0)
            lanes = at(side * tiles + j)

            def source(i, carry):
                rows = pl.ds(pl.multiple_of(i * group, group), group)
                parts = []
                for n in range(group // TILE):
                    tile = i * (group // TILE) + n
                    first_weight = ((tile * 2 + side) * tiles + j) * 4 * tiles + u * tiles
                    blocks = []
                    for k in range(tiles):
                        lane = pl.multiple_of(u * depth + k * 2 * TILE, 2 * TILE)
                        piece = lhs[pl.ds(pl.multiple_of(tile * TILE, TILE), TILE), pl.ds(lane, 2 * TILE)]
                        weight = w_ref[first_weight + k]
                        blocks.append((piece.astype(jnp.float32) * weight).astype(jnp.bfloat16))
                    parts.append(jnp.concatenate(blocks, axis=1))
                scaled = jnp.concatenate(parts, axis=0)
                product = jnp.dot(scaled, rhs[...], preferred_element_type=jnp.float32)
                if first:
                    out_ref[0, rows, lanes] = product[:, :TILE]
                    out_ref[1, rows, lanes] = product[:, TILE:]
                else:
                    out_ref[0, rows, lanes] += product[:, :TILE]
                    out_ref[1, rows, lanes] += product[:, TILE:]
                return carry

            lax.fori_loop(0, strip // group, source, 0)
            return carry

        lax.fori_loop(0, tiles, column, 0)

    def stair(u, i):
        return place(u, u, (i * band, band), (i * band, strip - i * band))

    def own_stair(i):
        return own(s, (i * band, band), (i * band, strip - i * band))

    def load_diagonal(u):
        for i in range(4):
            load(stair(u, i), (i * band, band), (i * band, strip - i * band))

    def own_place(core):
        return g_ref.at[
            :,
            pl.ds(pl.multiple_of(s * strip, strip), strip),
            pl.ds(pl.multiple_of(core * 2 * strip, strip), 2 * strip),
        ]

    def load_mixed():
        load(place(a, b, lower), rows=(0, half))
        load(place(b, a, cols=upper), rows=(half, strip), cols=upper)

    lower, upper = (0, half), (half, half)
    barrier = pltpu.get_barrier_semaphore()
    for device in (to_x, to_y, to_sibling):
        pl.semaphore_signal(barrier, inc=1, device_id=device, device_id_type=pl.DeviceIdType.MESH)
    pl.semaphore_wait(barrier, 3)

    @pl.when(home)
    def _():
        sends = [
            copy(0, x_ref.at[0], own_place(r), to_sibling),
            copy(15, own_stair(1), stair(s, 1), to_x),
            copy(18, own_stair(0), stair(s, 0), to_y),
            copy(16, own_stair(2), stair(s, 2), to_x),
            copy(21, own_stair(3), stair(s, 3), to_y),
            copy(14, own_stair(0), stair(s, 0), to_x),
            copy(19, own_stair(1), stair(s, 1), to_y),
            copy(17, own_stair(3), stair(s, 3), to_x),
            copy(20, own_stair(2), stair(s, 2), to_y),
            copy(5, own(a), place(s, a), to_y),
        ]
        for send in sends:
            send.start()
        load(own(s))
        fill_left(s)
        multiply(s, s, "as is", True)
        load(own(a))
        fill_left(a)
        multiply(s, a, "as is", True)
        forwards = []
        for i in (1, 2):
            arrive(14 + i, stair(a, i), to_x)
            forwards.append(copy(21 + i, stair(a, i), stair(a, i), to_y))
            forwards[-1].start()
        multiply(a, s, "flip", False)
        arrive(0, own_place(1 - r), to_sibling)
        load(place(s, b))
        fill_left(b)
        multiply(b, s, "flip", False)
        arrive(9, place(b, a, cols=upper), to_y)
        share = copy(11, place(b, a, cols=upper), place(b, a, cols=upper), to_sibling)
        share.start()
        load(place(s, d))
        fill_left(d)
        multiply(d, s, "flip", False)
        arrive(14, stair(a, 0), to_x)
        arrive(17, stair(a, 3), to_x)
        load_diagonal(a)
        multiply(a, a, "diagonal", False)
        arrive(12, place(a, d), to_sibling)
        load(place(a, d))
        multiply(d, a, "flip", False)
        arrive(13, place(a, b, lower), to_sibling)
        load_mixed()
        multiply(b, a, "mixed home", False)
        for send in sends + forwards + [share]:
            send.wait_send()

    @pl.when(jnp.logical_not(home))
    def _():
        sends = [
            copy(0, x_ref.at[0], own_place(r), to_sibling),
            copy(9, own(d, cols=upper), place(s, d, cols=upper), to_y),
            copy(7, own(b), place(s, b), to_x),
            copy(8, own(d, lower), place(s, d, lower), to_x),
        ]
        for send in sends:
            send.start()
        arrive(0, own_place(1 - r), to_sibling)
        load(place(s, a))
        fill_left(a)
        load(place(s, s))
        fill_left(s)
        forwards = []
        for n, i in enumerate((0, 3)):
            arrive(18 + i, stair(b, i), to_y)
            forwards.append(copy(24 + n, stair(b, i), stair(b, i), to_x))
            forwards[-1].start()
        load(own(b))
        fill_left(b)
        multiply(s, b, "as is", True)
        load(own(d))
        fill_left(d)
        multiply(s, d, "as is", True)
        arrive(19, stair(b, 1), to_y)
        arrive(20, stair(b, 2), to_y)
        load_diagonal(b)
        multiply(b, b, "diagonal", False)
        arrive(7, place(a, d), to_x)
        share = copy(12, place(a, d), place(a, d), to_sibling)
        share.start()
        load(place(a, d))
        multiply(a, d, "as is", False)
        arrive(8, place(a, b, lower), to_x)
        share_half = copy(13, place(a, b, lower), place(a, b, lower), to_sibling)
        share_half.start()
        arrive(11, place(b, a, cols=upper), to_sibling)
        load_mixed()
        multiply(a, b, "mixed other", False)
        arrive(5, place(b, d), to_y)
        load(place(b, d))
        multiply(b, d, "as is", False)
        multiply(d, b, "flip", False)
        arrive(22, stair(d, 1), to_y)
        arrive(23, stair(d, 2), to_y)
        arrive(24, stair(d, 0), to_x)
        arrive(25, stair(d, 3), to_x)
        load_diagonal(d)
        multiply(d, d, "diagonal", False)
        for send in sends + forwards + [share, share_half]:
            send.wait_send()


def fused(recorded, weights):
    rows, cols = recorded.shape[2], recorded.shape[3]
    whole = 4 * rows
    out, _ = pl.pallas_call(
        fused_kernel,
        out_shape=(
            jax.ShapeDtypeStruct((2, rows, cols), jnp.float32),
            jax.ShapeDtypeStruct((2, whole, whole), recorded.dtype),
        ),
        in_specs=[pl.BlockSpec(memory_space=pl.ANY), pl.BlockSpec(memory_space=pltpu.SMEM)],
        out_specs=(pl.BlockSpec(memory_space=pltpu.VMEM), pl.BlockSpec(memory_space=pl.ANY)),
        scratch_shapes=[
            pltpu.VMEM((rows, 2 * whole), jnp.bfloat16),
            pltpu.VMEM((2, rows + rows // 2, rows), jnp.bfloat16),
            pltpu.VMEM((2 * rows, 2 * TILE), jnp.bfloat16),
            pltpu.SemaphoreType.DMA((COPIES,)),
            pltpu.SemaphoreType.DMA((COPIES,)),
            pltpu.SemaphoreType.DMA,
        ],
        compiler_params=pltpu.CompilerParams(
            collective_id=0, has_side_effects=True, vmem_limit_bytes=60 * 1024 * 1024
        ),
        cost_estimate=pl.CostEstimate(
            flops=8 * rows * cols * whole, bytes_accessed=40 * rows * whole, transcendentals=0
        ),
        name="exchange_and_multiply",
    )(recorded, weights)
    return out


def tile_weights(aperture, blocks):
    offset = jnp.arange(blocks, dtype=jnp.int32)[None, None, :] - aperture[..., 0:1]
    extent = aperture[..., 1:2]
    margin = jnp.minimum(offset, extent - 1 - offset)
    ramp = (margin + 1).astype(jnp.float32) / (aperture[..., 2:3] + 1).astype(jnp.float32)
    return jnp.where((offset >= 0) & (offset < extent), jnp.minimum(1.0, ramp), 0.0)


def apply_kernel(
    row_tiles, col_tiles, blocks, mixed, aperture, straight, places, left_ref, *refs
):
    if mixed:
        column_ref, row_ref, out_ref, lhs, rhs, acc = refs
    else:
        column_ref, out_ref, lhs, rhs, acc = refs
    j = pl.program_id(0)

    def span(block, count):
        return pl.ds(pl.multiple_of(block * (2 * TILE), 2 * TILE), count * 2 * TILE)

    @pl.when(j == 0)
    def _():
        def interleave(k, carry):
            for c in range(2):
                lhs[:, pl.ds(pl.multiple_of((2 * k + c) * TILE, TILE), TILE)] = left_ref[
                    c, :, pl.ds(pl.multiple_of(k * TILE, TILE), TILE)
                ]
            return carry

        lax.fori_loop(0, blocks, interleave, 0)

    def build(k, carry):
        here = pl.ds(pl.multiple_of(k * TILE, TILE), TILE)
        first = pl.ds(pl.multiple_of(k * 2 * TILE, TILE), TILE)
        second = pl.ds(pl.multiple_of(k * 2 * TILE + TILE, TILE), TILE)

        def fill(real, imag):
            rhs[first, :TILE] = real
            rhs[first, TILE:] = imag
            rhs[second, :TILE] = -imag
            rhs[second, TILE:] = real

        if not mixed:
            fill(column_ref[0, here, :], column_ref[1, here, :])
            return carry
        as_is = straight[k * col_tiles + j] == 1

        @pl.when(as_is)
        def _():
            fill(column_ref[0, here, :], column_ref[1, here, :])

        @pl.when(jnp.logical_not(as_is))
        def _():
            fill(row_ref[0, :, here].T, row_ref[1, :, here].T)

        return carry

    lax.fori_loop(0, blocks, build, 0)

    def source_tile(i, carry):
        rows = pl.ds(pl.multiple_of(i * TILE, TILE), TILE)
        field = (i * col_tiles + j) * 3
        lo, extent, taper = aperture[field], aperture[field + 1], aperture[field + 2]
        acc[...] = jnp.zeros_like(acc)
        position = lo + taper
        inner = extent - 2 * taper
        size = 1
        while size * 2 <= blocks:
            size *= 2
        while size:
            present = lax.rem(inner // size, 2)

            @pl.when(present == 1)
            def _(size=size, position=position):
                part = span(position, size)
                acc[...] += jnp.dot(
                    lhs[rows, part], rhs[part, :], preferred_element_type=jnp.float32
                )

            position = position + present * size
            size //= 2
        for width in (1, 2):

            @pl.when(taper == width)
            def _(width=width):
                total = acc[...]
                for p in range(width):
                    weight = np.float32(p + 1) / np.float32(width + 1)
                    for block in (lo + p, lo + extent - 1 - p):
                        part = span(block, 1)
                        scaled = (lhs[rows, part].astype(jnp.float32) * weight).astype(jnp.bfloat16)
                        total += jnp.dot(scaled, rhs[part, :], preferred_element_type=jnp.float32)
                acc[...] = total

        out_ref[0, rows, :] = acc[:, :TILE]
        out_ref[1, rows, :] = acc[:, TILE:]
        return carry

    lax.fori_loop(0, row_tiles, source_tile, 0)


def apply(aperture, straight, places, left, column, row, own_rows, own_cols):
    whole = column.shape[1]
    blocks = whole // TILE
    row_tiles, col_tiles = own_rows // TILE, own_cols // TILE
    mixed = row is not None
    in_specs = [
        pl.BlockSpec(
            (2, own_rows, whole), lambda j, f, h, p: (0, p[0], 0), pipeline_mode=pl.Buffered(1)
        ),
        pl.BlockSpec((2, whole, TILE), lambda j, f, h, p: (0, 0, p[1] + j)),
    ]
    operands = [left, column]
    if mixed:
        in_specs.append(pl.BlockSpec((2, TILE, whole), lambda j, f, h, p: (0, p[1] + j, 0)))
        operands.append(row)
    flops = 8 * own_rows * own_cols * whole
    return pl.pallas_call(
        functools.partial(apply_kernel, row_tiles, col_tiles, blocks, mixed),
        out_shape=jax.ShapeDtypeStruct((2, own_rows, own_cols), jnp.float32),
        grid_spec=pltpu.PrefetchScalarGridSpec(
            num_scalar_prefetch=3,
            grid=(col_tiles,),
            in_specs=in_specs,
            out_specs=pl.BlockSpec((2, own_rows, TILE), lambda j, f, h, p: (0, 0, j)),
            scratch_shapes=[
                pltpu.VMEM((own_rows, 2 * whole), jnp.bfloat16),
                pltpu.VMEM((2 * whole, 2 * TILE), jnp.bfloat16),
                pltpu.VMEM((TILE, 2 * TILE), jnp.float32),
            ],
        ),
        compiler_params=pltpu.CompilerParams(vmem_limit_bytes=58 * 1024 * 1024),
        cost_estimate=pl.CostEstimate(
            flops=flops, bytes_accessed=40 * own_rows * whole, transcendentals=0
        ),
        name="apply_apertures",
    )(aperture.reshape(-1), straight.reshape(-1), places, *operands)


def shards(square, recorded, aperture):
    own_rows, own_cols = recorded.shape[2], recorded.shape[3]
    row_tiles, col_tiles = own_rows // TILE, own_cols // TILE
    if square:
        weights = tile_weights(aperture, 4 * row_tiles)
        out = fused(recorded, weights.reshape(-1))
        return out[None]
    places = jnp.zeros((2,), jnp.int32)
    straight = jnp.ones((1,), jnp.int32)
    left = lax.all_gather(recorded, "rcv", axis=3, tiled=True)
    column = lax.all_gather(recorded, "src", axis=2, tiled=True)
    outs = [
        apply(aperture, straight, places, left[f], column[f], None, own_rows, own_cols)
        for f in range(recorded.shape[0])
    ]
    return jnp.stack(outs)


def solution(mesh):
    square = mesh.shape["src"] == 4 and mesh.shape["rcv"] == 2
    in_specs = (P("grp", None, "src", "rcv"), P(("grp", "src"), "rcv", None))
    out_specs = P("grp", None, "src", "rcv")
    return jax.shard_map(
        functools.partial(shards, square),
        mesh=mesh,
        in_specs=in_specs,
        out_specs=out_specs,
        check_vma=False,
    )
```
